32 devices in a mesh: pair: 8 (over z, y), aux: 4 (over x, core).
Axes of the slice: x: 2, y: 2, z: 4, core: 2. Of those that a mesh axis runs over, the one named last changes fastest.
Arguments:
- three_center: bfloat16 [1024, 32, 2048], P(('pair', 'aux')), may hold values from -1 to 1
- panel: bfloat16 [512, 64], P('pair'), may hold values from -6 to 6
- metric: float32 [32, 64, 64], P(('pair', 'aux')), may hold values from -0.5 to 1.6
- screen: int32 [8, 128, 1], P(None, 'aux'), may hold values from 0 to 7; in each aligned block of 32 rows (0 to 31, 32 to 63, ..., all dimensions but the last counted through in order) at most 8 rows name the same one
- pair_blocks: int32 [8, 128, 2], P(None, 'aux'), may hold values from 0 to 15
Outputs:
- fitted: bfloat16 [32, 512, 4096], P(('pair', 'aux'))
- exchange: float32 [512, 512], P(('pair', 'aux'))
The draws below stay inside these ranges and needn't reach their ends.
Inputs may be any that keep to these rules, and one draw needn't show every extreme that they name: `screen`: in the list of one device no pair index is named by more than 8 slots, and in some lists one is named exactly 8 times.
All inputs are finite; a program needn't handle non-finite values.
Results may differ from the reference program's by a relative error of at most 0.0049.
Values may be sent and summed in bfloat16 or wider, within the bound.
A program may use at most 192 MiB of HBM per device.

```python
import math
import jax
import jax.numpy as jnp
import numpy as np
from jax import lax

FB = 32
NBLK = 16
AB = 64
OCC = 64
SLOTS = 32
CAP = 8
NBF = 512
NQ = 32
N_PAIR = 8
N_AUX = 4


def draw_metric(key, part):
    first_key, second_key = jax.random.split(key)
    indices = jnp.arange(AB)
    diagonal_mask = indices[:, None] == indices[None, :]
    offdiag = jax.random.normal(first_key, (NQ, AB, AB), jnp.float32) * (0.5 / math.sqrt(AB))
    diagonal = jax.random.uniform(second_key, (NQ, AB, AB), jnp.float32, 0.8, 1.2)
    offdiag = jnp.clip(offdiag, -0.5, 0.5)
    return jnp.where(diagonal_mask[None, :, :], diagonal, offdiag)


def touch_ends(array, key, smallest, high):
    spot = [jax.random.randint(jax.random.fold_in(key, axis), (), 0, length) for axis, length in enumerate(array.shape)]
    widest = array.shape.index(max(array.shape))
    next_to = spot[:widest] + [(spot[widest] + 1) % array.shape[widest]] + spot[widest + 1:]
    return array.at[tuple(spot)].set(smallest).at[tuple(next_to)].set(high)


def levels(stream_key, dims, pieces, least, largest):
    level = 1.0
    for axis_at, blocks in pieces:
        draws = jax.random.uniform(jax.random.fold_in(jax.random.fold_in(stream_key, 6), axis_at), (blocks,), jnp.float32, least / len(pieces), largest / len(pieces))
        level = level * jnp.repeat(jnp.exp(draws), dims[axis_at] // blocks).reshape((-1,) + (1,) * (len(dims) - 1 - axis_at))
    return level


def shared_out(rng, own, number, rows, number_of, top, most, skew):
    sequence = jax.random.permutation(rng, number_of)
    crowded, ordinary = portions_of(number_of, rows * top, most, skew, True), portions_of(number_of, rows * top, most, skew, False)
    places = jnp.arange(number_of)

    def named(lengths, offset_by):
        used = int((lengths > 0).sum())
        fixed = max(1, used // 4)
        moved = fixed + (places - fixed + offset_by * (used - fixed)) % max(1, number_of - fixed)
        return jnp.zeros((number_of,), jnp.int32).at[sequence[jnp.where(places < fixed, places, moved)]].set(jnp.asarray(lengths, jnp.int32))

    lengths = jnp.where(number % 4 == 0, named(crowded, number // 4), named(ordinary, number - number // 4 - 1))
    mixed = jax.random.permutation(jax.random.fold_in(own, 3), number_of)
    donor, receiver = mixed[0:number_of // 2 * 2:2], mixed[1:number_of // 2 * 2:2]
    room = jnp.minimum(lengths[donor] - 1, most - lengths[receiver]) // 2
    room = jnp.where((donor == sequence[0]) | (receiver == sequence[0]) | (lengths[receiver] == 0), 0, jnp.maximum(room, 0))
    moved = jax.random.randint(jax.random.fold_in(own, 4), (number_of // 2,), 0, 1 << 20) % (room + 1)
    lengths = lengths.at[donor].add(-moved).at[receiver].add(moved)
    members = jnp.searchsorted(jnp.cumsum(lengths), jnp.arange(rows * top), side="right").astype(jnp.int32)
    grid = members.reshape(top, rows).T
    grid = grid[jax.random.permutation(jax.random.fold_in(own, 1), rows)]
    offset_by = jax.random.randint(jax.random.fold_in(own, 2), (rows, 1), 0, top)
    return jnp.take_along_axis(grid, (jnp.arange(top)[None, :] + offset_by) % top, axis=1)


def portions_of(amount, total, bound, slope, full):
    portions = [(1 << 20) // math.isqrt(grade ** slope) + 1 for grade in range(1, amount + 1)]
    largest = bound if full else min(bound, max(-(-total // amount), total * portions[0] // sum(portions)))
    least = 1 if total - largest >= amount - 1 else 0
    holding, surplus = [largest] + [least] * (amount - 1), total - largest - least * (amount - 1)
    while surplus > 0:
        free = [i for i in range(1, amount) if holding[i] < largest] or [i for i in range(1, amount) if holding[i] < bound]
        mass, left = sum([portions[i] for i in free]), surplus
        for i in free:
            extra = min(bound - holding[i], max(1, left * portions[i] // mass), surplus)
            holding[i] = holding[i] + extra
            surplus = surplus - extra
    return np.array(holding)


def noise(stream_key, extent, scale, limit, cuts=(), held_as=jnp.bfloat16):
    array = jax.random.normal(stream_key, extent, jnp.float32) * scale
    if len(cuts) > 0:
        array = levels(stream_key, extent, cuts, -0.22, 0.18) * array
    return jnp.clip(array, min=-limit, max=limit).astype(held_as)


def setup_inputs(seed: int = 0) -> dict:
    key_of = jax.random.split(jax.random.key(seed), 6)
    three_center = noise(key_of[0], (N_PAIR * N_AUX * SLOTS, FB, AB * FB), FB ** -0.5, 1.0, ((0, 32),))
    panel = noise(key_of[1], (NBF, OCC), 1.0, 6.0, ((0, 8),))
    metric = draw_metric(jax.random.fold_in(key_of[5], 71), 0)
    screen_keys = jax.random.split(jax.random.fold_in(key_of[3], 1), N_PAIR * (N_AUX * SLOTS) // SLOTS)
    screen_turns = jax.random.permutation(jax.random.fold_in(key_of[3], 3), N_PAIR * (N_AUX * SLOTS) // SLOTS)
    screen = jax.vmap(lambda own, number: shared_out(jax.random.fold_in(key_of[3], 2), own, number, SLOTS, N_PAIR, 1, CAP, 2))(screen_keys, screen_turns).reshape((N_PAIR, N_AUX * SLOTS, 1))
    pair_blocks = touch_ends(jax.random.randint(key_of[4], (N_PAIR, N_AUX * SLOTS, 2), 0, NBLK), jax.random.fold_in(key_of[4], 1), 0, NBLK - 1).astype(jnp.int32)
    return {"three_center": three_center, "panel": panel, "metric": metric, "screen": screen, "pair_blocks": pair_blocks}


def reference(three_center, panel, metric, screen, pair_blocks):
    basis_total = NBLK * FB
    integrals = three_center.reshape(N_PAIR, N_AUX, SLOTS, FB, AB, FB)
    integrals = jnp.moveaxis(integrals, 1, 0).reshape(N_AUX, N_PAIR * SLOTS, FB, AB, FB)
    targets = jnp.moveaxis(screen.reshape(N_PAIR, N_AUX, SLOTS), 1, 0).reshape(N_AUX, N_PAIR * SLOTS)
    block_ids = jnp.moveaxis(pair_blocks.reshape(N_PAIR, N_AUX, SLOTS, 2), 1, 0).reshape(N_AUX, N_PAIR * SLOTS, 2)
    factors = jnp.moveaxis(metric.reshape(N_PAIR, N_AUX, AB, AB), 1, 0)
    panel_blocks = panel.astype(jnp.float32).reshape(NBLK, FB, OCC)

    def column(accumulated, inputs):
        column_ints, column_targets, column_blocks, column_factors = inputs
        picked = panel_blocks[column_blocks[:, 1]]
        transformed = jnp.einsum('smqn,sni->smqi', column_ints.astype(jnp.float32), picked)
        transformed = lax.optimization_barrier(transformed.astype(jnp.bfloat16)).astype(jnp.float32)
        segment_ids = (column_targets * NBLK + column_blocks[:, 0]).astype(jnp.int32)
        summed = jax.ops.segment_sum(transformed, segment_ids, num_segments=N_PAIR * NBLK)
        summed = summed.reshape(N_PAIR, basis_total, AB, OCC)
        fitted = jnp.einsum('dpq,drqi->drpi', column_factors, summed, precision=lax.Precision.HIGHEST)
        fitted = fitted.astype(jnp.bfloat16).reshape(N_PAIR, basis_total, AB * OCC)
        widened = fitted.astype(jnp.float32)
        column_sum = jnp.einsum('drx,dcx->rc', widened, widened)
        return accumulated + column_sum, fitted

    start_value = jnp.zeros((basis_total, basis_total), jnp.float32)
    accumulated, fitted_all = lax.scan(column, start_value, (integrals, targets, block_ids, factors))
    fitted_all = jnp.moveaxis(fitted_all, 0, 1).reshape(N_PAIR * N_AUX, basis_total, AB * OCC)
    norm_factor = 1.0 / (N_PAIR * N_AUX * AB * OCC)
    return fitted_all, accumulated * norm_factor
```

```python
import functools

import jax
import jax.numpy as jnp
from jax import lax
from jax.experimental import pallas as pl
from jax.experimental.pallas import tpu as pltpu
from jax.sharding import PartitionSpec as P

MESH = pl.DeviceIdType.MESH
QG = 8
IG = 16


def pack_kernel(pair_count, capacity, base, table_ref, tc_ref, packed_ref, counts, sems):
    me = lax.axis_index("pair")
    slot_count = tc_ref.shape[0]

    def clear(i, _):
        counts[i] = 0
        return 0

    lax.fori_loop(0, pair_count, clear, 0)

    def start(s, _):
        target = lax.div(table_ref[me, s], base * base)
        rank = counts[target]
        counts[target] = rank + 1
        pltpu.make_async_copy(
            tc_ref.at[s], packed_ref.at[target * capacity + rank], sems.at[s]
        ).start()
        return 0

    lax.fori_loop(0, slot_count, start, 0)

    def finish(s, _):
        pltpu.make_async_copy(tc_ref.at[s], packed_ref.at[0], sems.at[s]).wait()
        return 0

    lax.fori_loop(0, slot_count, finish, 0)


def exchange_kernel(n, packed_ref, recv_ref, send_sems, recv_sems, own_sem):
    me = lax.axis_index("pair")
    barrier = pltpu.get_barrier_semaphore()
    for k in range(1, n):
        pl.semaphore_signal(
            barrier, inc=1, device_id={"pair": lax.rem(me + k, n)}, device_id_type=MESH
        )
    pl.semaphore_wait(barrier, n - 1)
    copies = []
    for k in range(1, n):
        dst = lax.rem(me + k, n)
        copy = pltpu.make_async_remote_copy(
            src_ref=packed_ref.at[dst],
            dst_ref=recv_ref.at[me],
            send_sem=send_sems.at[k],
            recv_sem=recv_sems.at[k],
            device_id={"pair": dst},
            device_id_type=MESH,
        )
        copy.start()
        copies.append(copy)
    own = pltpu.make_async_copy(packed_ref.at[me], recv_ref.at[me], own_sem)
    own.start()
    own.wait()
    for copy in copies:
        copy.wait()


def iota(shape, axis):
    return lax.broadcasted_iota(jnp.int32, shape, axis)


def fit_kernel(
    capacity,
    table_ref,
    panel_ref,
    metric_ref,
    recv_ref,
    fitted_ref,
    gram_ref,
    recv_buf,
    weights,
    metric_hi,
    metric_lo,
    coeff,
    entries,
    recv_sem,
):
    me = lax.axis_index("pair")
    pair_count, slot_count = table_ref.shape
    width = recv_buf.shape[1]
    aux = metric_ref.shape[1]
    orbitals = panel_ref.shape[1]
    basis = panel_ref.shape[0]
    block_count = basis // width
    chunks = aux // QG
    groups = orbitals // IG
    depth = QG * width
    wide = QG * orbitals
    lanes = QG * IG

    load = pltpu.make_async_copy(recv_ref, recv_buf, recv_sem)
    load.start()

    def per_source(p, found):
        def per_slot(s, carry):
            found, rank = carry
            code = table_ref[p, s]
            mine = lax.div(code, block_count * block_count) == me

            @pl.when(mine)
            def _():
                entries[0, found] = p * capacity + rank
                entries[1, found] = lax.rem(lax.div(code, block_count), block_count)
                entries[2, found] = lax.rem(code, block_count)

            step = mine.astype(jnp.int32)
            return found + step, rank + step

        found, _ = lax.fori_loop(0, slot_count, per_slot, (found, 0))
        return found

    found = lax.fori_loop(0, pair_count, per_source, 0)
    entries[0, found] = 0
    entries[1, found] = block_count
    entries[2, found] = 0

    expand = (
        iota((orbitals, wide), 0) == iota((orbitals, wide), 1) // QG
    ).astype(jnp.bfloat16)
    diagonal = iota((depth, wide), 0) // width == iota((depth, wide), 1) % QG
    for n in range(block_count):
        block = panel_ref[n * width : (n + 1) * width, :]
        spread = jnp.dot(block, expand, preferred_element_type=jnp.float32)
        spread = jnp.concatenate([spread] * QG, axis=0)
        weights[n] = jnp.where(diagonal, spread, 0.0).astype(jnp.bfloat16)

    size = aux * IG
    metric = metric_ref[0]
    high = metric.astype(jnp.bfloat16)
    low = (metric - high.astype(jnp.float32)).astype(jnp.bfloat16)
    row_aux = (iota((size, aux), 0) // lanes) * QG + iota((size, aux), 0) % QG
    pick_row = (row_aux == iota((size, aux), 1)).astype(jnp.bfloat16)
    pick_col = (iota((aux, size), 0) == iota((aux, size), 1) // IG).astype(jnp.bfloat16)
    same = (iota((size, size), 0) % lanes) // QG == iota((size, size), 1) % IG
    for part, out in ((high, metric_hi), (low, metric_lo)):
        rows = lax.dot_general(
            pick_row, part, (((1,), (1,)), ((), ())), preferred_element_type=jnp.float32
        ).astype(jnp.bfloat16)
        full = jnp.dot(rows, pick_col, preferred_element_type=jnp.float32)
        out[...] = jnp.where(same, full, 0.0).astype(jnp.bfloat16)

    coeff[...] = jnp.zeros_like(coeff)
    load.wait()

    def add(k):
        entry, mu, nu = entries[0, k], entries[1, k], entries[2, k]
        block = recv_buf[entry]
        stacked = jnp.concatenate(
            [block[:, c * depth : (c + 1) * depth] for c in range(chunks)], axis=0
        )
        half = jnp.dot(stacked, weights[nu], preferred_element_type=jnp.float32)
        rows = pl.ds(pl.multiple_of(mu * width, width), width)
        for c in range(chunks):
            coeff[c, rows, :] += half[c * width : (c + 1) * width, :]

    def add_two(j, _):
        add(2 * j)
        add(2 * j + 1)
        return 0

    lax.fori_loop(0, (found + 1) // 2, add_two, 0)

    source = iota((wide, wide), 0)
    dest = iota((wide, wide), 1)
    wanted = (
        (dest % orbitals) // IG * lanes + dest // orbitals * IG + dest % IG
    )
    order = (source == wanted).astype(jnp.bfloat16)
    step = min(256, basis)
    for r in range(0, basis, step):
        parts = []
        for g in range(groups):
            piece = jnp.concatenate(
                [coeff[c, r : r + step, g * lanes : (g + 1) * lanes] for c in range(chunks)],
                axis=1,
            ).astype(jnp.bfloat16)
            out = jnp.dot(piece, metric_hi[...], preferred_element_type=jnp.float32)
            out += jnp.dot(piece, metric_lo[...], preferred_element_type=jnp.float32)
            parts.append(out.astype(jnp.bfloat16))
        for o in range(chunks):
            mixed = jnp.concatenate(
                [part[:, o * lanes : (o + 1) * lanes] for part in parts], axis=1
            )
            fitted_ref[0, r : r + step, o * wide : (o + 1) * wide] = jnp.dot(
                mixed, order, preferred_element_type=jnp.float32
            ).astype(jnp.bfloat16)
    gram_ref[...] = lax.dot_general(
        fitted_ref[0],
        fitted_ref[0],
        (((1,), (1,)), ((), ())),
        preferred_element_type=jnp.float32,
    )


def shards(three_center, panel, metric, screen, pair_blocks):
    pair_count = lax.axis_size("pair")
    column_count = lax.axis_size("aux")
    slot_count, width, flat = three_center.shape
    aux = metric.shape[1]
    orbitals = panel.shape[1]
    capacity = max(2, 2 * slot_count // pair_count)
    rows = pair_count * capacity
    whole_panel = lax.all_gather(panel, "pair", axis=0, tiled=True)
    basis = whole_panel.shape[0]
    block_count = basis // width
    table = (screen[:, :, 0] * block_count + pair_blocks[:, :, 0]) * block_count
    table += pair_blocks[:, :, 1]
    smem = pl.BlockSpec(memory_space=pltpu.SMEM)
    vmem = pl.BlockSpec(memory_space=pltpu.VMEM)
    hbm = pl.BlockSpec(memory_space=pl.ANY)

    packed = pl.pallas_call(
        functools.partial(pack_kernel, pair_count, capacity, block_count),
        out_shape=jax.ShapeDtypeStruct((rows, width, flat), jnp.bfloat16),
        in_specs=[smem, hbm],
        out_specs=hbm,
        scratch_shapes=[
            pltpu.SMEM((pair_count,), jnp.int32),
            pltpu.SemaphoreType.DMA((slot_count,)),
        ],
        name="pack",
    )(table, three_center)

    received = pl.pallas_call(
        functools.partial(exchange_kernel, pair_count),
        out_shape=jax.ShapeDtypeStruct((pair_count, capacity, width, flat), jnp.bfloat16),
        in_specs=[hbm],
        out_specs=hbm,
        scratch_shapes=[
            pltpu.SemaphoreType.DMA((pair_count,)),
            pltpu.SemaphoreType.DMA((pair_count,)),
            pltpu.SemaphoreType.DMA,
        ],
        compiler_params=pltpu.CompilerParams(collective_id=0, has_side_effects=True),
        name="exchange_blocks",
    )(packed.reshape(pair_count, capacity, width, flat))

    size = aux * IG
    fitted, gram = pl.pallas_call(
        functools.partial(fit_kernel, capacity),
        out_shape=(
            jax.ShapeDtypeStruct((1, basis, aux * orbitals), jnp.bfloat16),
            jax.ShapeDtypeStruct((basis, basis), jnp.float32),
        ),
        in_specs=[smem, vmem, vmem, hbm],
        out_specs=(vmem, vmem),
        scratch_shapes=[
            pltpu.VMEM((rows, width, flat), jnp.bfloat16),
            pltpu.VMEM((block_count, QG * width, QG * orbitals), jnp.bfloat16),
            pltpu.VMEM((size, size), jnp.bfloat16),
            pltpu.VMEM((size, size), jnp.bfloat16),
            pltpu.VMEM((aux // QG, basis + width, QG * orbitals), jnp.float32),
            pltpu.SMEM((3, rows + 8), jnp.int32),
            pltpu.SemaphoreType.DMA,
        ],
        compiler_params=pltpu.CompilerParams(vmem_limit_bytes=44 * 2**20),
        name="fit",
    )(table, whole_panel, metric, received.reshape(rows, width, flat))

    summed_rows = lax.psum_scatter(gram, ("pair", "aux"), scatter_dimension=0, tiled=True)
    norm_factor = 1.0 / (pair_count * column_count * aux * orbitals)
    return fitted, summed_rows * norm_factor


def solution(mesh):
    return jax.shard_map(
        shards,
        mesh=mesh,
        in_specs=(
            P(("pair", "aux"), None, None),
            P("pair", None),
            P(("pair", "aux"), None, None),
            P(None, "aux", None),
            P(None, "aux", None),
        ),
        out_specs=(P(("pair", "aux"), None, None), P(("pair", "aux"), None)),
        check_vma=False,
    )
```

```python
import functools

import jax
import jax.numpy as jnp
from jax import lax
from jax.experimental import pallas as pl
from jax.experimental.pallas import tpu as pltpu
from jax.sharding import PartitionSpec as P

MESH = pl.DeviceIdType.MESH
QG = 8
IG = 16


def pack_kernel(pair_count, capacity, base, table_ref, tc_ref, packed_ref, counts, sems):
    me = lax.axis_index("pair")
    slot_count = tc_ref.shape[0]

    def clear(i, _):
        counts[i] = 0
        return 0

    lax.fori_loop(0, pair_count, clear, 0)

    def start(s, _):
        target = lax.div(table_ref[me, s], base * base)
        rank = counts[target]
        counts[target] = rank + 1
        pltpu.make_async_copy(
            tc_ref.at[s], packed_ref.at[target * capacity + rank], sems.at[s]
        ).start()
        return 0

    lax.fori_loop(0, slot_count, start, 0)

    def finish(s, _):
        pltpu.make_async_copy(tc_ref.at[s], packed_ref.at[0], sems.at[s]).wait()
        return 0

    lax.fori_loop(0, slot_count, finish, 0)


def exchange_kernel(
    n,
    packed_ref,
    panel_ref,
    recv_ref,
    whole_ref,
    send_sems,
    recv_sems,
    panel_send,
    panel_recv,
    own_sem,
):
    me = lax.axis_index("pair")
    rows = panel_ref.shape[0]
    mine = pl.ds(pl.multiple_of(me * rows, rows), rows)
    barrier = pltpu.get_barrier_semaphore()
    for k in range(1, n):
        pl.semaphore_signal(
            barrier, inc=1, device_id={"pair": lax.rem(me + k, n)}, device_id_type=MESH
        )
    pl.semaphore_wait(barrier, n - 1)
    copies = []
    for k in range(1, n):
        copy = pltpu.make_async_remote_copy(
            src_ref=panel_ref,
            dst_ref=whole_ref.at[mine],
            send_sem=panel_send.at[k],
            recv_sem=panel_recv.at[k],
            device_id={"pair": lax.rem(me + k, n)},
            device_id_type=MESH,
        )
        copy.start()
        copies.append(copy)
    for k in range(1, n):
        dst = lax.rem(me + k, n)
        copy = pltpu.make_async_remote_copy(
            src_ref=packed_ref.at[dst],
            dst_ref=recv_ref.at[me],
            send_sem=send_sems.at[k],
            recv_sem=recv_sems.at[k],
            device_id={"pair": dst},
            device_id_type=MESH,
        )
        copy.start()
        copies.append(copy)
    own = pltpu.make_async_copy(packed_ref.at[me], recv_ref.at[me], own_sem)
    own.start()
    whole_ref[mine, :] = panel_ref[...]
    own.wait()
    for copy in copies:
        copy.wait()


def iota(shape, axis):
    return lax.broadcasted_iota(jnp.int32, shape, axis)


def fit_kernel(
    capacity,
    table_ref,
    panel_ref,
    metric_ref,
    recv_ref,
    fitted_ref,
    gram_ref,
    recv_buf,
    weights,
    metric_hi,
    metric_lo,
    coeff,
    entries,
    recv_sem,
):
    me = lax.axis_index("pair")
    pair_count, slot_count = table_ref.shape
    width = recv_buf.shape[1]
    aux = metric_ref.shape[1]
    orbitals = panel_ref.shape[1]
    basis = panel_ref.shape[0]
    block_count = basis // width
    chunks = aux // QG
    groups = orbitals // IG
    depth = QG * width
    wide = QG * orbitals
    lanes = QG * IG

    load = pltpu.make_async_copy(recv_ref, recv_buf, recv_sem)
    load.start()

    def per_source(p, found):
        def per_slot(s, carry):
            found, rank = carry
            code = table_ref[p, s]
            mine = lax.div(code, block_count * block_count) == me

            @pl.when(mine)
            def _():
                entries[0, found] = p * capacity + rank
                entries[1, found] = lax.rem(lax.div(code, block_count), block_count)
                entries[2, found] = lax.rem(code, block_count)

            step = mine.astype(jnp.int32)
            return found + step, rank + step

        found, _ = lax.fori_loop(0, slot_count, per_slot, (found, 0))
        return found

    found = lax.fori_loop(0, pair_count, per_source, 0)
    entries[0, found] = 0
    entries[1, found] = block_count
    entries[2, found] = 0

    expand = (
        iota((orbitals, wide), 0) == iota((orbitals, wide), 1) // QG
    ).astype(jnp.bfloat16)
    diagonal = iota((depth, wide), 0) // width == iota((depth, wide), 1) % QG
    for n in range(block_count):
        block = panel_ref[n * width : (n + 1) * width, :]
        spread = jnp.dot(block, expand, preferred_element_type=jnp.float32)
        spread = jnp.concatenate([spread] * QG, axis=0)
        weights[n] = jnp.where(diagonal, spread, 0.0).astype(jnp.bfloat16)

    size = aux * IG
    metric = metric_ref[0]
    high = metric.astype(jnp.bfloat16)
    low = (metric - high.astype(jnp.float32)).astype(jnp.bfloat16)
    row_aux = (iota((size, aux), 0) // lanes) * QG + iota((size, aux), 0) % QG
    pick_row = (row_aux == iota((size, aux), 1)).astype(jnp.bfloat16)
    pick_col = (iota((aux, size), 0) == iota((aux, size), 1) // IG).astype(jnp.bfloat16)
    same = (iota((size, size), 0) % lanes) // QG == iota((size, size), 1) % IG
    for part, out in ((high, metric_hi), (low, metric_lo)):
        rows = lax.dot_general(
            pick_row, part, (((1,), (1,)), ((), ())), preferred_element_type=jnp.float32
        ).astype(jnp.bfloat16)
        full = jnp.dot(rows, pick_col, preferred_element_type=jnp.float32)
        out[...] = jnp.where(same, full, 0.0).astype(jnp.bfloat16)

    coeff[...] = jnp.zeros_like(coeff)
    load.wait()

    def add(k):
        entry, mu, nu = entries[0, k], entries[1, k], entries[2, k]
        block = recv_buf[entry]
        stacked = jnp.concatenate(
            [block[:, c * depth : (c + 1) * depth] for c in range(chunks)], axis=0
        )
        half = jnp.dot(stacked, weights[nu], preferred_element_type=jnp.float32)
        rows = pl.ds(pl.multiple_of(mu * width, width), width)
        for c in range(chunks):
            coeff[c, rows, :] += half[c * width : (c + 1) * width, :]

    def add_two(j, _):
        add(2 * j)
        add(2 * j + 1)
        return 0

    lax.fori_loop(0, (found + 1) // 2, add_two, 0)

    source = iota((wide, wide), 0)
    dest = iota((wide, wide), 1)
    wanted = (
        (dest % orbitals) // IG * lanes + dest // orbitals * IG + dest % IG
    )
    order = (source == wanted).astype(jnp.bfloat16)
    step = min(256, basis)
    for r in range(0, basis, step):
        parts = []
        for g in range(groups):
            piece = jnp.concatenate(
                [coeff[c, r : r + step, g * lanes : (g + 1) * lanes] for c in range(chunks)],
                axis=1,
            ).astype(jnp.bfloat16)
            out = jnp.dot(piece, metric_hi[...], preferred_element_type=jnp.float32)
            out += jnp.dot(piece, metric_lo[...], preferred_element_type=jnp.float32)
            parts.append(out.astype(jnp.bfloat16))
        for o in range(chunks):
            mixed = jnp.concatenate(
                [part[:, o * lanes : (o + 1) * lanes] for part in parts], axis=1
            )
            fitted_ref[0, r : r + step, o * wide : (o + 1) * wide] = jnp.dot(
                mixed, order, preferred_element_type=jnp.float32
            ).astype(jnp.bfloat16)
    gram_ref[...] = lax.dot_general(
        fitted_ref[0],
        fitted_ref[0],
        (((1,), (1,)), ((), ())),
        preferred_element_type=jnp.float32,
    )


def reduce_kernel(
    n,
    columns,
    norm_factor,
    gram_ref,
    out_ref,
    send_one,
    recv_one,
    partial,
    send_two,
    recv_two,
    send_one_sems,
    recv_one_sems,
    send_two_sems,
    recv_two_sems,
):
    me = lax.axis_index("pair")
    col = lax.axis_index("aux")
    barrier = pltpu.get_barrier_semaphore()
    for k in range(1, columns):
        pl.semaphore_signal(
            barrier, inc=1, device_id={"aux": lax.rem(col + k, columns)}, device_id_type=MESH
        )
    for k in range(1, n):
        pl.semaphore_signal(
            barrier, inc=1, device_id={"pair": lax.rem(me + k, n)}, device_id_type=MESH
        )
    for a in range(columns):
        send_one[a] = gram_ref[:, a].astype(send_one.dtype)
    pl.semaphore_wait(barrier, columns + n - 2)
    copies = []
    for k in range(1, columns):
        dst = lax.rem(col + k, columns)
        copy = pltpu.make_async_remote_copy(
            src_ref=send_one.at[dst],
            dst_ref=recv_one.at[k - 1],
            send_sem=send_one_sems.at[k],
            recv_sem=recv_one_sems.at[k],
            device_id={"aux": dst},
            device_id_type=MESH,
        )
        copy.start()
        copies.append(copy)
    total = gram_ref[:, col]
    for k, copy in enumerate(copies):
        copy.wait()
        total += recv_one[k].astype(jnp.float32)
    partial[...] = total
    send_two[...] = total.astype(send_two.dtype)
    copies = []
    for k in range(1, n):
        dst = lax.rem(me + k, n)
        copy = pltpu.make_async_remote_copy(
            src_ref=send_two.at[dst],
            dst_ref=recv_two.at[k - 1],
            send_sem=send_two_sems.at[k],
            recv_sem=recv_two_sems.at[k],
            device_id={"pair": dst},
            device_id_type=MESH,
        )
        copy.start()
        copies.append(copy)
    total = partial[me]
    for k, copy in enumerate(copies):
        copy.wait()
        total += recv_two[k].astype(jnp.float32)
    out_ref[...] = total * norm_factor


def shards(three_center, panel, metric, screen, pair_blocks):
    pair_count = lax.axis_size("pair")
    column_count = lax.axis_size("aux")
    slot_count, width, flat = three_center.shape
    aux = metric.shape[1]
    orbitals = panel.shape[1]
    capacity = max(2, 2 * slot_count // pair_count)
    rows = pair_count * capacity
    basis = pair_count * panel.shape[0]
    block_count = basis // width
    table = (screen[:, :, 0] * block_count + pair_blocks[:, :, 0]) * block_count
    table += pair_blocks[:, :, 1]
    smem = pl.BlockSpec(memory_space=pltpu.SMEM)
    vmem = pl.BlockSpec(memory_space=pltpu.VMEM)
    hbm = pl.BlockSpec(memory_space=pl.ANY)

    packed = pl.pallas_call(
        functools.partial(pack_kernel, pair_count, capacity, block_count),
        out_shape=jax.ShapeDtypeStruct((rows, width, flat), jnp.bfloat16),
        in_specs=[smem, hbm],
        out_specs=vmem,
        scratch_shapes=[
            pltpu.SMEM((pair_count,), jnp.int32),
            pltpu.SemaphoreType.DMA((slot_count,)),
        ],
        compiler_params=pltpu.CompilerParams(vmem_limit_bytes=16 * 2**20),
        name="pack",
    )(table, three_center)

    received, whole_panel = pl.pallas_call(
        functools.partial(exchange_kernel, pair_count),
        out_shape=(
            jax.ShapeDtypeStruct((pair_count, capacity, width, flat), jnp.bfloat16),
            jax.ShapeDtypeStruct((basis, orbitals), jnp.bfloat16),
        ),
        in_specs=[hbm, vmem],
        out_specs=(hbm, vmem),
        scratch_shapes=[
            pltpu.SemaphoreType.DMA((pair_count,)),
            pltpu.SemaphoreType.DMA((pair_count,)),
            pltpu.SemaphoreType.DMA((pair_count,)),
            pltpu.SemaphoreType.DMA((pair_count,)),
            pltpu.SemaphoreType.DMA,
        ],
        compiler_params=pltpu.CompilerParams(collective_id=0, has_side_effects=True),
        name="exchange_blocks",
    )(packed.reshape(pair_count, capacity, width, flat), panel)

    size = aux * IG
    fitted, gram = pl.pallas_call(
        functools.partial(fit_kernel, capacity),
        out_shape=(
            jax.ShapeDtypeStruct((1, basis, aux * orbitals), jnp.bfloat16),
            jax.ShapeDtypeStruct((basis, basis), jnp.float32),
        ),
        in_specs=[smem, vmem, vmem, hbm],
        out_specs=(vmem, vmem),
        scratch_shapes=[
            pltpu.VMEM((rows, width, flat), jnp.bfloat16),
            pltpu.VMEM((block_count, QG * width, QG * orbitals), jnp.bfloat16),
            pltpu.VMEM((size, size), jnp.bfloat16),
            pltpu.VMEM((size, size), jnp.bfloat16),
            pltpu.VMEM((aux // QG, basis + width, QG * orbitals), jnp.float32),
            pltpu.SMEM((3, rows + 8), jnp.int32),
            pltpu.SemaphoreType.DMA,
        ],
        compiler_params=pltpu.CompilerParams(vmem_limit_bytes=44 * 2**20),
        name="fit",
    )(table, whole_panel, metric, received.reshape(rows, width, flat))

    norm_factor = 1.0 / (pair_count * column_count * aux * orbitals)
    part = basis // (pair_count * column_count)
    exchange = pl.pallas_call(
        functools.partial(reduce_kernel, pair_count, column_count, norm_factor),
        out_shape=jax.ShapeDtypeStruct((part, basis), jnp.float32),
        in_specs=[vmem],
        out_specs=vmem,
        scratch_shapes=[
            pltpu.VMEM((column_count, pair_count, part, basis), jnp.bfloat16),
            pltpu.VMEM((column_count - 1, pair_count, part, basis), jnp.bfloat16),
            pltpu.VMEM((pair_count, part, basis), jnp.float32),
            pltpu.VMEM((pair_count, part, basis), jnp.bfloat16),
            pltpu.VMEM((pair_count - 1, part, basis), jnp.bfloat16),
            pltpu.SemaphoreType.DMA((column_count,)),
            pltpu.SemaphoreType.DMA((column_count,)),
            pltpu.SemaphoreType.DMA((pair_count,)),
            pltpu.SemaphoreType.DMA((pair_count,)),
        ],
        compiler_params=pltpu.CompilerParams(
            collective_id=1, has_side_effects=True, vmem_limit_bytes=24 * 2**20
        ),
        name="reduce_rows",
    )(gram.reshape(pair_count, column_count, part, basis))
    return fitted, exchange


def solution(mesh):
    return jax.shard_map(
        shards,
        mesh=mesh,
        in_specs=(
            P(("pair", "aux"), None, None),
            P("pair", None),
            P(("pair", "aux"), None, None),
            P(None, "aux", None),
            P(None, "aux", None),
        ),
        out_specs=(P(("pair", "aux"), None, None), P(("pair", "aux"), None)),
        check_vma=False,
    )
```

```python
import functools

import jax
import jax.numpy as jnp
from jax import lax
from jax.experimental import pallas as pl
from jax.experimental.pallas import tpu as pltpu
from jax.sharding import PartitionSpec as P

MESH = pl.DeviceIdType.MESH
QG = 8
IG = 16


def pack_kernel(
    pair_count, capacity, base, table_ref, tc_ref, packed_ref, entries, counts, sems
):
    me = lax.axis_index("pair")
    slot_count = tc_ref.shape[0]
    rows = packed_ref.shape[0]

    def clear(i, _):
        counts[i] = 0
        return 0

    lax.fori_loop(0, pair_count, clear, 0)

    def start(s, _):
        target = lax.div(table_ref[me, s], base * base)
        rank = counts[target]
        counts[target] = rank + 1
        pltpu.make_async_copy(
            tc_ref.at[s], packed_ref.at[target * capacity + rank], sems.at[s]
        ).start()
        return 0

    lax.fori_loop(0, slot_count, start, 0)

    def per_source(p, found):
        def per_slot(s, carry):
            found, rank = carry
            code = table_ref[p, s]
            mine = lax.div(code, base * base) == me

            @pl.when(mine)
            def _():
                entries[0, found] = p * capacity + rank
                entries[1, found] = lax.rem(lax.div(code, base), base)
                entries[2, found] = lax.rem(code, base)

            step = mine.astype(jnp.int32)
            return found + step, rank + step

        found, _ = lax.fori_loop(0, slot_count, per_slot, (found, 0))
        return found

    found = lax.fori_loop(0, pair_count, per_source, 0)
    entries[0, found] = 0
    entries[1, found] = base
    entries[2, found] = 0
    entries[0, rows + 1] = found

    def finish(s, _):
        pltpu.make_async_copy(tc_ref.at[s], packed_ref.at[0], sems.at[s]).wait()
        return 0

    lax.fori_loop(0, slot_count, finish, 0)


def iota(shape, axis):
    return lax.broadcasted_iota(jnp.int32, shape, axis)


def build_weights(panel_ref, metric_ref, weights, metric_hi, metric_lo):
    aux = metric_ref.shape[1]
    orbitals = panel_ref.shape[1]
    block_count, depth, wide = weights.shape
    width = depth // QG
    lanes = QG * IG
    expand = (
        iota((orbitals, wide), 0) == iota((orbitals, wide), 1) // QG
    ).astype(jnp.bfloat16)
    diagonal = iota((depth, wide), 0) // width == iota((depth, wide), 1) % QG
    for n in range(block_count):
        block = panel_ref[n * width : (n + 1) * width, :]
        spread = jnp.dot(block, expand, preferred_element_type=jnp.float32)
        spread = jnp.concatenate([spread] * QG, axis=0)
        weights[n] = jnp.where(diagonal, spread, 0.0).astype(jnp.bfloat16)

    size = aux * IG
    metric = metric_ref[0]
    high = metric.astype(jnp.bfloat16)
    low = (metric - high.astype(jnp.float32)).astype(jnp.bfloat16)
    row_aux = (iota((size, aux), 0) // lanes) * QG + iota((size, aux), 0) % QG
    pick_row = (row_aux == iota((size, aux), 1)).astype(jnp.bfloat16)
    pick_col = (iota((aux, size), 0) == iota((aux, size), 1) // IG).astype(jnp.bfloat16)
    same = (iota((size, size), 0) % lanes) // QG == iota((size, size), 1) % IG
    for part, out in ((high, metric_hi), (low, metric_lo)):
        rows = lax.dot_general(
            pick_row, part, (((1,), (1,)), ((), ())), preferred_element_type=jnp.float32
        ).astype(jnp.bfloat16)
        full = jnp.dot(rows, pick_col, preferred_element_type=jnp.float32)
        out[...] = jnp.where(same, full, 0.0).astype(jnp.bfloat16)


def exchange_kernel(
    n,
    packed_ref,
    panel_ref,
    metric_ref,
    recv_ref,
    weights,
    metric_hi,
    metric_lo,
    whole_ref,
    send_sems,
    recv_sems,
    panel_send,
    panel_recv,
    own_sem,
):
    me = lax.axis_index("pair")
    rows = panel_ref.shape[0]
    mine = pl.ds(pl.multiple_of(me * rows, rows), rows)
    barrier = pltpu.get_barrier_semaphore()
    for k in range(1, n):
        pl.semaphore_signal(
            barrier, inc=1, device_id={"pair": lax.rem(me + k, n)}, device_id_type=MESH
        )
    pl.semaphore_wait(barrier, n - 1)
    panels = []
    for k in range(1, n):
        copy = pltpu.make_async_remote_copy(
            src_ref=panel_ref,
            dst_ref=whole_ref.at[mine],
            send_sem=panel_send.at[k],
            recv_sem=panel_recv.at[k],
            device_id={"pair": lax.rem(me + k, n)},
            device_id_type=MESH,
        )
        copy.start()
        panels.append(copy)
    copies = []
    for k in sorted(range(1, n), key=lambda k: abs(2 * k - n)):
        dst = lax.rem(me + k, n)
        copy = pltpu.make_async_remote_copy(
            src_ref=packed_ref.at[dst],
            dst_ref=recv_ref.at[me],
            send_sem=send_sems.at[k],
            recv_sem=recv_sems.at[k],
            device_id={"pair": dst},
            device_id_type=MESH,
        )
        copy.start()
        copies.append(copy)
    own = pltpu.make_async_copy(packed_ref.at[me], recv_ref.at[me], own_sem)
    own.start()
    whole_ref[mine, :] = panel_ref[...]
    for copy in panels:
        copy.wait()
    build_weights(whole_ref, metric_ref, weights, metric_hi, metric_lo)
    own.wait()
    for copy in copies:
        copy.wait()


def fit_kernel(
    block_count,
    orbitals,
    entries,
    weights,
    metric_hi,
    metric_lo,
    recv_buf,
    fitted_ref,
    gram_ref,
    coeff,
):
    width = recv_buf.shape[1]
    basis = block_count * width
    chunks, _, wide = coeff.shape
    groups = orbitals // IG
    depth = QG * width
    lanes = QG * IG
    found = entries[0, recv_buf.shape[0] + 1]
    coeff[...] = jnp.zeros_like(coeff)

    def add(k):
        entry, mu, nu = entries[0, k], entries[1, k], entries[2, k]
        block = recv_buf[entry]
        stacked = jnp.concatenate(
            [block[:, c * depth : (c + 1) * depth] for c in range(chunks)], axis=0
        )
        half = jnp.dot(stacked, weights[nu], preferred_element_type=jnp.float32)
        rows = pl.ds(pl.multiple_of(mu * width, width), width)
        for c in range(chunks):
            coeff[c, rows, :] += half[c * width : (c + 1) * width, :]

    def add_two(j, _):
        add(2 * j)
        add(2 * j + 1)
        return 0

    lax.fori_loop(0, (found + 1) // 2, add_two, 0)

    source = iota((wide, wide), 0)
    dest = iota((wide, wide), 1)
    wanted = (
        (dest % orbitals) // IG * lanes + dest // orbitals * IG + dest % IG
    )
    order = (source == wanted).astype(jnp.bfloat16)
    step = min(256, basis)
    for r in range(0, basis, step):
        parts = []
        for g in range(groups):
            piece = jnp.concatenate(
                [coeff[c, r : r + step, g * lanes : (g + 1) * lanes] for c in range(chunks)],
                axis=1,
            ).astype(jnp.bfloat16)
            out = jnp.dot(piece, metric_hi[...], preferred_element_type=jnp.float32)
            out += jnp.dot(piece, metric_lo[...], preferred_element_type=jnp.float32)
            parts.append(out.astype(jnp.bfloat16))
        for o in range(chunks):
            mixed = jnp.concatenate(
                [part[:, o * lanes : (o + 1) * lanes] for part in parts], axis=1
            )
            fitted_ref[0, r : r + step, o * wide : (o + 1) * wide] = jnp.dot(
                mixed, order, preferred_element_type=jnp.float32
            ).astype(jnp.bfloat16)
    gram_ref[...] = lax.dot_general(
        fitted_ref[0],
        fitted_ref[0],
        (((1,), (1,)), ((), ())),
        preferred_element_type=jnp.float32,
    )


def reduce_kernel(
    n,
    columns,
    norm_factor,
    gram_ref,
    out_ref,
    send_one,
    recv_one,
    partial,
    send_two,
    recv_two,
    send_one_sems,
    recv_one_sems,
    send_two_sems,
    recv_two_sems,
):
    me = lax.axis_index("pair")
    col = lax.axis_index("aux")
    barrier = pltpu.get_barrier_semaphore()
    for k in range(1, columns):
        pl.semaphore_signal(
            barrier, inc=1, device_id={"aux": lax.rem(col + k, columns)}, device_id_type=MESH
        )
    for k in range(1, n):
        pl.semaphore_signal(
            barrier, inc=1, device_id={"pair": lax.rem(me + k, n)}, device_id_type=MESH
        )
    for a in range(columns):
        send_one[a] = gram_ref[:, a].astype(send_one.dtype)
    pl.semaphore_wait(barrier, columns + n - 2)
    copies = []
    for k in range(1, columns):
        dst = lax.rem(col + k, columns)
        copy = pltpu.make_async_remote_copy(
            src_ref=send_one.at[dst],
            dst_ref=recv_one.at[k - 1],
            send_sem=send_one_sems.at[k],
            recv_sem=recv_one_sems.at[k],
            device_id={"aux": dst},
            device_id_type=MESH,
        )
        copy.start()
        copies.append(copy)
    total = gram_ref[:, col]
    for k, copy in enumerate(copies):
        copy.wait()
        total += recv_one[k].astype(jnp.float32)
    partial[...] = total
    send_two[...] = total.astype(send_two.dtype)
    copies = []
    for k in range(1, n):
        dst = lax.rem(me + k, n)
        copy = pltpu.make_async_remote_copy(
            src_ref=send_two.at[dst],
            dst_ref=recv_two.at[k - 1],
            send_sem=send_two_sems.at[k],
            recv_sem=recv_two_sems.at[k],
            device_id={"pair": dst},
            device_id_type=MESH,
        )
        copy.start()
        copies.append(copy)
    total = partial[me]
    for k, copy in enumerate(copies):
        copy.wait()
        total += recv_two[k].astype(jnp.float32)
    out_ref[...] = total * norm_factor


def shards(three_center, panel, metric, screen, pair_blocks):
    pair_count = lax.axis_size("pair")
    column_count = lax.axis_size("aux")
    slot_count, width, flat = three_center.shape
    aux = metric.shape[1]
    orbitals = panel.shape[1]
    capacity = max(2, 2 * slot_count // pair_count)
    rows = pair_count * capacity
    basis = pair_count * panel.shape[0]
    block_count = basis // width
    table = (screen[:, :, 0] * block_count + pair_blocks[:, :, 0]) * block_count
    table += pair_blocks[:, :, 1]
    smem = pl.BlockSpec(memory_space=pltpu.SMEM)
    vmem = pl.BlockSpec(memory_space=pltpu.VMEM)
    hbm = pl.BlockSpec(memory_space=pl.ANY)

    size = aux * IG
    depth, wide = QG * width, QG * orbitals

    packed, entries = pl.pallas_call(
        functools.partial(pack_kernel, pair_count, capacity, block_count),
        out_shape=(
            jax.ShapeDtypeStruct((rows, width, flat), jnp.bfloat16),
            jax.ShapeDtypeStruct((3, rows + 2), jnp.int32),
        ),
        in_specs=[smem, hbm],
        out_specs=(vmem, smem),
        scratch_shapes=[
            pltpu.SMEM((pair_count,), jnp.int32),
            pltpu.SemaphoreType.DMA((slot_count,)),
        ],
        compiler_params=pltpu.CompilerParams(vmem_limit_bytes=16 * 2**20),
        name="pack",
    )(table, three_center)

    received, weights, metric_hi, metric_lo = pl.pallas_call(
        functools.partial(exchange_kernel, pair_count),
        out_shape=(
            jax.ShapeDtypeStruct((pair_count, capacity, width, flat), jnp.bfloat16),
            jax.ShapeDtypeStruct((block_count, depth, wide), jnp.bfloat16),
            jax.ShapeDtypeStruct((size, size), jnp.bfloat16),
            jax.ShapeDtypeStruct((size, size), jnp.bfloat16),
        ),
        in_specs=[vmem, vmem, vmem],
        out_specs=(vmem, vmem, vmem, vmem),
        scratch_shapes=[
            pltpu.VMEM((basis, orbitals), jnp.bfloat16),
            pltpu.SemaphoreType.DMA((pair_count,)),
            pltpu.SemaphoreType.DMA((pair_count,)),
            pltpu.SemaphoreType.DMA((pair_count,)),
            pltpu.SemaphoreType.DMA((pair_count,)),
            pltpu.SemaphoreType.DMA,
        ],
        compiler_params=pltpu.CompilerParams(
            collective_id=0, has_side_effects=True, vmem_limit_bytes=28 * 2**20
        ),
        name="exchange_blocks",
    )(packed.reshape(pair_count, capacity, width, flat), panel, metric)

    fitted, gram = pl.pallas_call(
        functools.partial(fit_kernel, block_count, orbitals),
        out_shape=(
            jax.ShapeDtypeStruct((1, basis, aux * orbitals), jnp.bfloat16),
            jax.ShapeDtypeStruct((basis, basis), jnp.float32),
        ),
        in_specs=[smem, vmem, vmem, vmem, vmem],
        out_specs=(vmem, vmem),
        scratch_shapes=[
            pltpu.VMEM((aux // QG, basis + width, wide), jnp.float32),
        ],
        compiler_params=pltpu.CompilerParams(vmem_limit_bytes=36 * 2**20),
        name="fit",
    )(entries, weights, metric_hi, metric_lo, received.reshape(rows, width, flat))

    norm_factor = 1.0 / (pair_count * column_count * aux * orbitals)
    part = basis // (pair_count * column_count)
    exchange = pl.pallas_call(
        functools.partial(reduce_kernel, pair_count, column_count, norm_factor),
        out_shape=jax.ShapeDtypeStruct((part, basis), jnp.float32),
        in_specs=[vmem],
        out_specs=vmem,
        scratch_shapes=[
            pltpu.VMEM((column_count, pair_count, part, basis), jnp.bfloat16),
            pltpu.VMEM((column_count - 1, pair_count, part, basis), jnp.bfloat16),
            pltpu.VMEM((pair_count, part, basis), jnp.float32),
            pltpu.VMEM((pair_count, part, basis), jnp.bfloat16),
            pltpu.VMEM((pair_count - 1, part, basis), jnp.bfloat16),
            pltpu.SemaphoreType.DMA((column_count,)),
            pltpu.SemaphoreType.DMA((column_count,)),
            pltpu.SemaphoreType.DMA((pair_count,)),
            pltpu.SemaphoreType.DMA((pair_count,)),
        ],
        compiler_params=pltpu.CompilerParams(
            collective_id=1, has_side_effects=True, vmem_limit_bytes=24 * 2**20
        ),
        name="reduce_rows",
    )(gram.reshape(pair_count, column_count, part, basis))
    return fitted, exchange


def solution(mesh):
    return jax.shard_map(
        shards,
        mesh=mesh,
        in_specs=(
            P(("pair", "aux"), None, None),
            P("pair", None),
            P(("pair", "aux"), None, None),
            P(None, "aux", None),
            P(None, "aux", None),
        ),
        out_specs=(P(("pair", "aux"), None, None), P(("pair", "aux"), None)),
        check_vma=False,
    )
```

```python
import functools

import jax
import jax.numpy as jnp
from jax import lax
from jax.experimental import pallas as pl
from jax.experimental.pallas import tpu as pltpu
from jax.sharding import PartitionSpec as P

MESH = pl.DeviceIdType.MESH
QG = 8
IG = 16


def pack_kernel(
    pair_count, capacity, spill, base, table_ref, tc_ref, packed_ref, entries, counts, sems
):
    me = lax.axis_index("pair")
    slot_count = tc_ref.shape[0]
    direct = pair_count * capacity
    last = entries.shape[1] - 1

    def clear(i, _):
        counts[i] = 0
        return 0

    lax.fori_loop(0, pair_count, clear, 0)

    def start(s, extra):
        target = lax.div(table_ref[me, s], base * base)
        rank = counts[target]
        counts[target] = rank + 1
        over = rank >= capacity
        place = jnp.where(over, direct + extra, target * capacity + rank)
        place = jnp.minimum(place, direct + spill - 1)
        pltpu.make_async_copy(tc_ref.at[s], packed_ref.at[place], sems.at[s]).start()
        return extra + over.astype(jnp.int32)

    lax.fori_loop(0, slot_count, start, 0)

    def per_source(p, found):
        lax.fori_loop(0, pair_count, clear, 0)

        def per_slot(s, carry):
            found, extra = carry
            code = table_ref[p, s]
            target = lax.div(code, base * base)
            rank = counts[target]
            counts[target] = rank + 1
            over = rank >= capacity
            mine = target == me

            @pl.when(mine)
            def _():
                entries[0, found] = jnp.where(
                    over, direct + p * spill + extra, p * capacity + rank
                )
                entries[1, found] = lax.rem(lax.div(code, base), base)
                entries[2, found] = lax.rem(code, base)

            return found + mine.astype(jnp.int32), extra + over.astype(jnp.int32)

        found, _ = lax.fori_loop(0, slot_count, per_slot, (found, 0))
        return found

    found = lax.fori_loop(0, pair_count, per_source, 0)
    entries[0, found] = 0
    entries[1, found] = base
    entries[2, found] = 0
    entries[0, last] = found

    def finish(s, _):
        pltpu.make_async_copy(tc_ref.at[s], packed_ref.at[0], sems.at[s]).wait()
        return 0

    lax.fori_loop(0, slot_count, finish, 0)


def iota(shape, axis):
    return lax.broadcasted_iota(jnp.int32, shape, axis)


def build_weights(panel_ref, metric_ref, weights, metric_hi, metric_lo):
    aux = metric_ref.shape[1]
    orbitals = panel_ref.shape[1]
    block_count, depth, wide = weights.shape
    width = depth // QG
    lanes = QG * IG
    expand = (
        iota((orbitals, wide), 0) == iota((orbitals, wide), 1) // QG
    ).astype(jnp.bfloat16)
    diagonal = iota((depth, wide), 0) // width == iota((depth, wide), 1) % QG
    for n in range(block_count):
        block = panel_ref[n * width : (n + 1) * width, :]
        spread = jnp.dot(block, expand, preferred_element_type=jnp.float32)
        spread = jnp.concatenate([spread] * QG, axis=0)
        weights[n] = jnp.where(diagonal, spread, 0.0).astype(jnp.bfloat16)

    size = aux * IG
    metric = metric_ref[0]
    high = metric.astype(jnp.bfloat16)
    low = (metric - high.astype(jnp.float32)).astype(jnp.bfloat16)
    row_aux = (iota((size, aux), 0) // lanes) * QG + iota((size, aux), 0) % QG
    pick_row = (row_aux == iota((size, aux), 1)).astype(jnp.bfloat16)
    pick_col = (iota((aux, size), 0) == iota((aux, size), 1) // IG).astype(jnp.bfloat16)
    same = (iota((size, size), 0) % lanes) // QG == iota((size, size), 1) % IG
    for part, out in ((high, metric_hi), (low, metric_lo)):
        rows = lax.dot_general(
            pick_row, part, (((1,), (1,)), ((), ())), preferred_element_type=jnp.float32
        ).astype(jnp.bfloat16)
        full = jnp.dot(rows, pick_col, preferred_element_type=jnp.float32)
        out[...] = jnp.where(same, full, 0.0).astype(jnp.bfloat16)


def exchange_kernel(
    n,
    capacity,
    spill,
    packed_ref,
    panel_ref,
    metric_ref,
    recv_ref,
    weights,
    metric_hi,
    metric_lo,
    whole_ref,
    send_sems,
    recv_sems,
    panel_send,
    panel_recv,
    own_sem,
    spill_sem,
    hop_send,
    hop_recv,
    side_send,
    side_recv,
):
    me = lax.axis_index("pair")
    rows = panel_ref.shape[0]
    mine = pl.ds(pl.multiple_of(me * rows, rows), rows)
    barrier = pltpu.get_barrier_semaphore()
    for k in range(1, n):
        pl.semaphore_signal(
            barrier, inc=1, device_id={"pair": lax.rem(me + k, n)}, device_id_type=MESH
        )
    pl.semaphore_wait(barrier, n - 1)
    panels = []
    for k in range(1, n):
        copy = pltpu.make_async_remote_copy(
            src_ref=panel_ref,
            dst_ref=whole_ref.at[mine],
            send_sem=panel_send.at[k],
            recv_sem=panel_recv.at[k],
            device_id={"pair": lax.rem(me + k, n)},
            device_id_type=MESH,
        )
        copy.start()
        panels.append(copy)
    direct = n * capacity
    own_spill = packed_ref.at[pl.ds(direct, spill)] if spill else None

    def landing(source):
        return recv_ref.at[pl.ds(direct + source * spill, spill)]

    def forward(source, dst, first, send_sem, recv_sem):
        return pltpu.make_async_remote_copy(
            src_ref=own_spill if first else landing(source),
            dst_ref=landing(source),
            send_sem=send_sem,
            recv_sem=recv_sem,
            device_id={"pair": dst},
            device_id_type=MESH,
        )

    length = n // 2
    at = lax.div(me, 2)
    other = me + 1 - 2 * lax.rem(me, 2)

    def hop(way, h):
        place = at if way else length - 1 - at
        step = 2 if way else -2
        sends = jnp.logical_and(place >= h, place < length - 1)
        copy = forward(
            jnp.clip(me - step * h, 0, n - 1),
            jnp.clip(me + step, 0, n - 1),
            h == 0,
            hop_send.at[way * length + h],
            hop_recv.at[way * length + h],
        )
        return copy, sends, place >= h + 1

    def side(source, first):
        place = lax.div(source, 2)
        return forward(source, other, first, side_send.at[place], side_recv.at[place])

    def start_hop(h):
        for way in (0, 1):
            copy, sends, _ = hop(way, h)
            pl.when(sends)(copy.start)

    def take_hop(h):
        for way in (0, 1):
            copy, _, arrives = hop(way, h)
            source = jnp.clip(me - (2 if way else -2) * (h + 1), 0, n - 1)

            @pl.when(arrives)
            def _():
                copy.wait_recv()
                side(source, False).start()

    own_copies = [
        pltpu.make_async_copy(
            packed_ref.at[pl.ds(me * capacity, capacity)],
            recv_ref.at[pl.ds(me * capacity, capacity)],
            own_sem,
        )
    ]
    if spill:
        own_copies.append(pltpu.make_async_copy(own_spill, landing(me), spill_sem))
        start_hop(0)
        side(me, True).start()
    copies = []
    for k in sorted(range(1, n), key=lambda k: abs(2 * k - n)):
        dst = lax.rem(me + k, n)
        copies.append(
            pltpu.make_async_remote_copy(
                src_ref=packed_ref.at[pl.ds(dst * capacity, capacity)],
                dst_ref=recv_ref.at[pl.ds(me * capacity, capacity)],
                send_sem=send_sems.at[k],
                recv_sem=recv_sems.at[k],
                device_id={"pair": dst},
                device_id_type=MESH,
            )
        )
    head = 2 if spill else n - 1
    for copy in copies[:head]:
        copy.start()
    for copy in own_copies:
        copy.start()
    whole_ref[mine, :] = panel_ref[...]
    for copy in panels:
        copy.wait()
    build_weights(whole_ref, metric_ref, weights, metric_hi, metric_lo)
    if spill:
        take_hop(0)
        for h in range(1, length - 1):
            start_hop(h)
            for copy in copies[head : head + 2]:
                copy.start()
            head += 2
            take_hop(h)
        for copy in copies[head:]:
            copy.start()
        for h in range(length - 1):
            for way in (0, 1):
                copy, sends, _ = hop(way, h)
                pl.when(sends)(copy.wait_send)
        for place in range(length):
            copy = forward(
                2 * place, other, False, side_send.at[place], side_recv.at[place]
            )
            copy.wait()
    for copy in own_copies:
        copy.wait()
    for copy in copies:
        copy.wait()


def flag_kernel(
    columns, targets_count, capacity, screen_ref, out_ref, send, recv, send_sems, recv_sems
):
    col = lax.axis_index("aux")
    barrier = pltpu.get_barrier_semaphore()
    for k in range(1, columns):
        pl.semaphore_signal(
            barrier, inc=1, device_id={"aux": lax.rem(col + k, columns)}, device_id_type=MESH
        )
    targets = screen_ref[...]
    beyond = jnp.zeros((targets.shape[0], 1), jnp.float32)
    for t in range(targets_count):
        named = jnp.sum(jnp.where(targets == t, 1.0, 0.0), axis=1, keepdims=True)
        beyond += jnp.maximum(named - capacity, 0.0)
    worst = jnp.zeros(out_ref.shape, jnp.float32) + jnp.max(beyond, axis=0, keepdims=True)
    send[...] = worst
    pl.semaphore_wait(barrier, columns - 1)
    copies = []
    for k in range(1, columns):
        copy = pltpu.make_async_remote_copy(
            src_ref=send,
            dst_ref=recv.at[k - 1],
            send_sem=send_sems.at[k],
            recv_sem=recv_sems.at[k],
            device_id={"aux": lax.rem(col + k, columns)},
            device_id_type=MESH,
        )
        copy.start()
        copies.append(copy)
    for k, copy in enumerate(copies):
        copy.wait()
        worst = jnp.maximum(worst, recv[k])
    out_ref[...] = worst


def fit_kernel(
    block_count,
    orbitals,
    entries,
    weights,
    metric_hi,
    metric_lo,
    recv_buf,
    fitted_ref,
    gram_ref,
    coeff,
):
    width = recv_buf.shape[1]
    basis = block_count * width
    chunks, _, wide = coeff.shape
    groups = orbitals // IG
    depth = QG * width
    lanes = QG * IG
    found = entries[0, entries.shape[1] - 1]
    coeff[...] = jnp.zeros_like(coeff)

    def add(k):
        entry, mu, nu = entries[0, k], entries[1, k], entries[2, k]
        block = recv_buf[entry]
        stacked = jnp.concatenate(
            [block[:, c * depth : (c + 1) * depth] for c in range(chunks)], axis=0
        )
        half = jnp.dot(stacked, weights[nu], preferred_element_type=jnp.float32)
        rows = pl.ds(pl.multiple_of(mu * width, width), width)
        for c in range(chunks):
            coeff[c, rows, :] += half[c * width : (c + 1) * width, :]

    def add_two(j, _):
        add(2 * j)
        add(2 * j + 1)
        return 0

    lax.fori_loop(0, (found + 1) // 2, add_two, 0)

    source = iota((wide, wide), 0)
    dest = iota((wide, wide), 1)
    wanted = (
        (dest % orbitals) // IG * lanes + dest // orbitals * IG + dest % IG
    )
    order = (source == wanted).astype(jnp.bfloat16)
    step = min(256, basis)
    for r in range(0, basis, step):
        parts = []
        for g in range(groups):
            piece = jnp.concatenate(
                [coeff[c, r : r + step, g * lanes : (g + 1) * lanes] for c in range(chunks)],
                axis=1,
            ).astype(jnp.bfloat16)
            out = jnp.dot(piece, metric_hi[...], preferred_element_type=jnp.float32)
            out += jnp.dot(piece, metric_lo[...], preferred_element_type=jnp.float32)
            parts.append(out.astype(jnp.bfloat16))
        for o in range(chunks):
            mixed = jnp.concatenate(
                [part[:, o * lanes : (o + 1) * lanes] for part in parts], axis=1
            )
            fitted_ref[0, r : r + step, o * wide : (o + 1) * wide] = jnp.dot(
                mixed, order, preferred_element_type=jnp.float32
            ).astype(jnp.bfloat16)
    gram_ref[...] = lax.dot_general(
        fitted_ref[0],
        fitted_ref[0],
        (((1,), (1,)), ((), ())),
        preferred_element_type=jnp.float32,
    )


def reduce_kernel(
    n,
    columns,
    norm_factor,
    gram_ref,
    out_ref,
    send_one,
    recv_one,
    partial,
    send_two,
    recv_two,
    send_one_sems,
    recv_one_sems,
    send_two_sems,
    recv_two_sems,
):
    me = lax.axis_index("pair")
    col = lax.axis_index("aux")
    barrier = pltpu.get_barrier_semaphore()
    for k in range(1, columns):
        pl.semaphore_signal(
            barrier, inc=1, device_id={"aux": lax.rem(col + k, columns)}, device_id_type=MESH
        )
    for k in range(1, n):
        pl.semaphore_signal(
            barrier, inc=1, device_id={"pair": lax.rem(me + k, n)}, device_id_type=MESH
        )
    for a in range(columns):
        send_one[a] = gram_ref[:, a].astype(send_one.dtype)
    pl.semaphore_wait(barrier, columns + n - 2)
    copies = []
    for k in range(1, columns):
        dst = lax.rem(col + k, columns)
        copy = pltpu.make_async_remote_copy(
            src_ref=send_one.at[dst],
            dst_ref=recv_one.at[k - 1],
            send_sem=send_one_sems.at[k],
            recv_sem=recv_one_sems.at[k],
            device_id={"aux": dst},
            device_id_type=MESH,
        )
        copy.start()
        copies.append(copy)
    total = gram_ref[:, col]
    for k, copy in enumerate(copies):
        copy.wait()
        total += recv_one[k].astype(jnp.float32)
    partial[...] = total
    send_two[...] = total.astype(send_two.dtype)
    copies = []
    for k in range(1, n):
        dst = lax.rem(me + k, n)
        copy = pltpu.make_async_remote_copy(
            src_ref=send_two.at[dst],
            dst_ref=recv_two.at[k - 1],
            send_sem=send_two_sems.at[k],
            recv_sem=recv_two_sems.at[k],
            device_id={"pair": dst},
            device_id_type=MESH,
        )
        copy.start()
        copies.append(copy)
    total = partial[me]
    for k, copy in enumerate(copies):
        copy.wait()
        total += recv_two[k].astype(jnp.float32)
    out_ref[...] = total * norm_factor


def shards(three_center, panel, metric, screen, pair_blocks):
    pair_count = lax.axis_size("pair")
    column_count = lax.axis_size("aux")
    slot_count, width, flat = three_center.shape
    aux = metric.shape[1]
    orbitals = panel.shape[1]
    capacity = max(2, 2 * slot_count // pair_count)
    rows = pair_count * capacity
    basis = pair_count * panel.shape[0]
    block_count = basis // width
    table = (screen[:, :, 0] * block_count + pair_blocks[:, :, 0]) * block_count
    table += pair_blocks[:, :, 1]
    smem = pl.BlockSpec(memory_space=pltpu.SMEM)
    vmem = pl.BlockSpec(memory_space=pltpu.VMEM)
    hbm = pl.BlockSpec(memory_space=pl.ANY)

    size = aux * IG
    depth, wide = QG * width, QG * orbitals

    def fit(part, spill, table, three_center, panel, metric):
        packed, entries = pl.pallas_call(
            functools.partial(pack_kernel, pair_count, part, spill, block_count),
            out_shape=(
                jax.ShapeDtypeStruct((pair_count * part + spill, width, flat), jnp.bfloat16),
                jax.ShapeDtypeStruct((3, rows + 2), jnp.int32),
            ),
            in_specs=[smem, hbm],
            out_specs=(vmem, smem),
            scratch_shapes=[
                pltpu.SMEM((pair_count,), jnp.int32),
                pltpu.SemaphoreType.DMA((slot_count,)),
            ],
            compiler_params=pltpu.CompilerParams(vmem_limit_bytes=16 * 2**20),
            name="pack",
        )(table, three_center)

        received, weights, metric_hi, metric_lo = pl.pallas_call(
            functools.partial(exchange_kernel, pair_count, part, spill),
            out_shape=(
                jax.ShapeDtypeStruct((pair_count * (part + spill), width, flat), jnp.bfloat16),
                jax.ShapeDtypeStruct((block_count, depth, wide), jnp.bfloat16),
                jax.ShapeDtypeStruct((size, size), jnp.bfloat16),
                jax.ShapeDtypeStruct((size, size), jnp.bfloat16),
            ),
            in_specs=[vmem, vmem, vmem],
            out_specs=(vmem, vmem, vmem, vmem),
            scratch_shapes=[
                pltpu.VMEM((basis, orbitals), jnp.bfloat16),
                pltpu.SemaphoreType.DMA((pair_count,)),
                pltpu.SemaphoreType.DMA((pair_count,)),
                pltpu.SemaphoreType.DMA((pair_count,)),
                pltpu.SemaphoreType.DMA((pair_count,)),
                pltpu.SemaphoreType.DMA,
                pltpu.SemaphoreType.DMA,
                pltpu.SemaphoreType.DMA((pair_count,)),
                pltpu.SemaphoreType.DMA((pair_count,)),
                pltpu.SemaphoreType.DMA((pair_count,)),
                pltpu.SemaphoreType.DMA((pair_count,)),
            ],
            compiler_params=pltpu.CompilerParams(
                collective_id=2 if spill else 0, has_side_effects=True, vmem_limit_bytes=28 * 2**20
            ),
            name="exchange_blocks",
        )(packed, panel, metric)

        fitted, gram = pl.pallas_call(
            functools.partial(fit_kernel, block_count, orbitals),
            out_shape=(
                jax.ShapeDtypeStruct((1, basis, aux * orbitals), jnp.bfloat16),
                jax.ShapeDtypeStruct((basis, basis), jnp.float32),
            ),
            in_specs=[smem, vmem, vmem, vmem, vmem],
            out_specs=(vmem, vmem),
            scratch_shapes=[
                pltpu.VMEM((aux // QG, basis + width, wide), jnp.float32),
            ],
            compiler_params=pltpu.CompilerParams(vmem_limit_bytes=33 * 2**20),
            name="fit",
        )(entries, weights, metric_hi, metric_lo, received)
        return fitted, gram

    arrays = (table, three_center, panel, metric)
    direct, spill = 5 * capacity // 8, 3 * slot_count // 16
    if capacity < 8 or pair_count % 2:
        fitted, gram = fit(capacity, 0, *arrays)
    else:
        worst = pl.pallas_call(
            functools.partial(flag_kernel, column_count, pair_count, direct),
            out_shape=jax.ShapeDtypeStruct((8, 128), jnp.float32),
            in_specs=[vmem],
            out_specs=vmem,
            scratch_shapes=[
                pltpu.VMEM((8, 128), jnp.float32),
                pltpu.VMEM((column_count - 1, 8, 128), jnp.float32),
                pltpu.SemaphoreType.DMA((column_count,)),
                pltpu.SemaphoreType.DMA((column_count,)),
            ],
            compiler_params=pltpu.CompilerParams(collective_id=3, has_side_effects=True),
            name="most_beyond",
        )(screen[:, :, 0])
        fitted, gram = lax.cond(
            worst[0, 0] <= spill,
            functools.partial(fit, direct, spill),
            functools.partial(fit, capacity, 0),
            *arrays,
        )

    norm_factor = 1.0 / (pair_count * column_count * aux * orbitals)
    part = basis // (pair_count * column_count)
    exchange = pl.pallas_call(
        functools.partial(reduce_kernel, pair_count, column_count, norm_factor),
        out_shape=jax.ShapeDtypeStruct((part, basis), jnp.float32),
        in_specs=[vmem],
        out_specs=vmem,
        scratch_shapes=[
            pltpu.VMEM((column_count, pair_count, part, basis), jnp.bfloat16),
            pltpu.VMEM((column_count - 1, pair_count, part, basis), jnp.bfloat16),
            pltpu.VMEM((pair_count, part, basis), jnp.float32),
            pltpu.VMEM((pair_count, part, basis), jnp.bfloat16),
            pltpu.VMEM((pair_count - 1, part, basis), jnp.bfloat16),
            pltpu.SemaphoreType.DMA((column_count,)),
            pltpu.SemaphoreType.DMA((column_count,)),
            pltpu.SemaphoreType.DMA((pair_count,)),
            pltpu.SemaphoreType.DMA((pair_count,)),
        ],
        compiler_params=pltpu.CompilerParams(
            collective_id=1, has_side_effects=True, vmem_limit_bytes=24 * 2**20
        ),
        name="reduce_rows",
    )(gram.reshape(pair_count, column_count, part, basis))
    return fitted, exchange


def solution(mesh):
    return jax.shard_map(
        shards,
        mesh=mesh,
        in_specs=(
            P(("pair", "aux"), None, None),
            P("pair", None),
            P(("pair", "aux"), None, None),
            P(None, "aux", None),
            P(None, "aux", None),
        ),
        out_specs=(P(("pair", "aux"), None, None), P(("pair", "aux"), None)),
        check_vma=False,
    )
```

```python
import functools

import jax
import jax.numpy as jnp
from jax import lax
from jax.experimental import pallas as pl
from jax.experimental.pallas import tpu as pltpu
from jax.sharding import PartitionSpec as P

MESH = pl.DeviceIdType.MESH
QG = 8
IG = 16


def pack_kernel(
    pair_count, capacity, spill, base, table_ref, tc_ref, packed_ref, entries, counts, sems
):
    me = lax.axis_index("pair")
    slot_count = tc_ref.shape[0]
    direct = pair_count * capacity
    last = entries.shape[1] - 1

    def clear(i, _):
        counts[i] = 0
        return 0

    lax.fori_loop(0, pair_count, clear, 0)

    def start(s, extra):
        target = lax.div(table_ref[me, s], base * base)
        rank = counts[target]
        counts[target] = rank + 1
        over = rank >= capacity
        place = jnp.where(over, direct + extra, target * capacity + rank)
        place = jnp.minimum(place, direct + spill - 1)
        pltpu.make_async_copy(tc_ref.at[s], packed_ref.at[place], sems.at[s]).start()
        return extra + over.astype(jnp.int32)

    lax.fori_loop(0, slot_count, start, 0)

    def per_source(p, found):
        lax.fori_loop(0, pair_count, clear, 0)

        def per_slot(s, carry):
            found, extra = carry
            code = table_ref[p, s]
            target = lax.div(code, base * base)
            rank = counts[target]
            counts[target] = rank + 1
            over = rank >= capacity
            mine = target == me

            @pl.when(mine)
            def _():
                entries[0, found] = jnp.where(
                    over, direct + p * spill + extra, p * capacity + rank
                )
                entries[1, found] = lax.rem(lax.div(code, base), base)
                entries[2, found] = lax.rem(code, base)

            return found + mine.astype(jnp.int32), extra + over.astype(jnp.int32)

        found, _ = lax.fori_loop(0, slot_count, per_slot, (found, 0))
        return found

    found = lax.fori_loop(0, pair_count, per_source, 0)
    entries[0, found] = 0
    entries[1, found] = base
    entries[2, found] = 0
    entries[0, last] = found

    def finish(s, _):
        pltpu.make_async_copy(tc_ref.at[s], packed_ref.at[0], sems.at[s]).wait()
        return 0

    lax.fori_loop(0, slot_count, finish, 0)


def iota(shape, axis):
    return lax.broadcasted_iota(jnp.int32, shape, axis)


def build_weights(panel_ref, metric_ref, weights, metric_hi, metric_lo):
    aux = metric_ref.shape[1]
    orbitals = panel_ref.shape[1]
    block_count, depth, wide = weights.shape
    width = depth // QG
    lanes = QG * IG
    expand = (
        iota((orbitals, wide), 0) == iota((orbitals, wide), 1) // QG
    ).astype(jnp.bfloat16)
    diagonal = iota((depth, wide), 0) // width == iota((depth, wide), 1) % QG
    for n in range(block_count):
        block = panel_ref[n * width : (n + 1) * width, :]
        spread = jnp.dot(block, expand, preferred_element_type=jnp.float32)
        spread = jnp.concatenate([spread] * QG, axis=0)
        weights[n] = jnp.where(diagonal, spread, 0.0).astype(jnp.bfloat16)

    size = aux * IG
    metric = metric_ref[0]
    high = metric.astype(jnp.bfloat16)
    low = (metric - high.astype(jnp.float32)).astype(jnp.bfloat16)
    row_aux = (iota((size, aux), 0) // lanes) * QG + iota((size, aux), 0) % QG
    pick_row = (row_aux == iota((size, aux), 1)).astype(jnp.bfloat16)
    pick_col = (iota((aux, size), 0) == iota((aux, size), 1) // IG).astype(jnp.bfloat16)
    same = (iota((size, size), 0) % lanes) // QG == iota((size, size), 1) % IG
    for part, out in ((high, metric_hi), (low, metric_lo)):
        rows = lax.dot_general(
            pick_row, part, (((1,), (1,)), ((), ())), preferred_element_type=jnp.float32
        ).astype(jnp.bfloat16)
        full = jnp.dot(rows, pick_col, preferred_element_type=jnp.float32)
        out[...] = jnp.where(same, full, 0.0).astype(jnp.bfloat16)


def exchange_kernel(
    n,
    capacity,
    spill,
    packed_ref,
    panel_ref,
    metric_ref,
    recv_ref,
    weights,
    metric_hi,
    metric_lo,
    whole_ref,
    send_sems,
    recv_sems,
    panel_send,
    panel_recv,
    own_sem,
    spill_sem,
    hop_send,
    hop_recv,
    side_send,
    side_recv,
):
    me = lax.axis_index("pair")
    rows = panel_ref.shape[0]
    mine = pl.ds(pl.multiple_of(me * rows, rows), rows)
    barrier = pltpu.get_barrier_semaphore()
    for k in range(1, n):
        pl.semaphore_signal(
            barrier, inc=1, device_id={"pair": lax.rem(me + k, n)}, device_id_type=MESH
        )
    pl.semaphore_wait(barrier, n - 1)
    panels = []
    for k in range(1, n):
        copy = pltpu.make_async_remote_copy(
            src_ref=panel_ref,
            dst_ref=whole_ref.at[mine],
            send_sem=panel_send.at[k],
            recv_sem=panel_recv.at[k],
            device_id={"pair": lax.rem(me + k, n)},
            device_id_type=MESH,
        )
        copy.start()
        panels.append(copy)
    direct = n * capacity
    own_spill = packed_ref.at[pl.ds(direct, spill)] if spill else None

    def landing(source):
        return recv_ref.at[pl.ds(direct + source * spill, spill)]

    def forward(source, dst, first, send_sem, recv_sem):
        return pltpu.make_async_remote_copy(
            src_ref=own_spill if first else landing(source),
            dst_ref=landing(source),
            send_sem=send_sem,
            recv_sem=recv_sem,
            device_id={"pair": dst},
            device_id_type=MESH,
        )

    length = n // 2
    at = lax.div(me, 2)
    other = me + 1 - 2 * lax.rem(me, 2)

    def hop(way, h):
        place = at if way else length - 1 - at
        step = 2 if way else -2
        sends = jnp.logical_and(place >= h, place < length - 1)
        copy = forward(
            jnp.clip(me - step * h, 0, n - 1),
            jnp.clip(me + step, 0, n - 1),
            h == 0,
            hop_send.at[way * length + h],
            hop_recv.at[way * length + h],
        )
        return copy, sends, place >= h + 1

    def side(source, first):
        place = lax.div(source, 2)
        return forward(source, other, first, side_send.at[place], side_recv.at[place])

    def start_hop(h):
        for way in (0, 1):
            copy, sends, _ = hop(way, h)
            pl.when(sends)(copy.start)

    def take_hop(h):
        for way in (0, 1):
            copy, _, arrives = hop(way, h)
            source = jnp.clip(me - (2 if way else -2) * (h + 1), 0, n - 1)

            @pl.when(arrives)
            def _():
                copy.wait_recv()
                side(source, False).start()

    own_copies = [
        pltpu.make_async_copy(
            packed_ref.at[pl.ds(me * capacity, capacity)],
            recv_ref.at[pl.ds(me * capacity, capacity)],
            own_sem,
        )
    ]
    if spill:
        own_copies.append(pltpu.make_async_copy(own_spill, landing(me), spill_sem))
        start_hop(0)
        side(me, True).start()
    copies = []
    for k in sorted(range(1, n), key=lambda k: abs(2 * k - n)):
        dst = lax.rem(me + k, n)
        copies.append(
            pltpu.make_async_remote_copy(
                src_ref=packed_ref.at[pl.ds(dst * capacity, capacity)],
                dst_ref=recv_ref.at[pl.ds(me * capacity, capacity)],
                send_sem=send_sems.at[k],
                recv_sem=recv_sems.at[k],
                device_id={"pair": dst},
                device_id_type=MESH,
            )
        )
    if not spill:
        for copy in copies:
            copy.start()
    for copy in own_copies:
        copy.start()
    whole_ref[mine, :] = panel_ref[...]
    for copy in panels:
        copy.wait()
    build_weights(whole_ref, metric_ref, weights, metric_hi, metric_lo)
    if spill:
        for h in range(1, length - 1):
            take_hop(h - 1)
            start_hop(h)
        for copy in copies:
            copy.start()
        if length > 1:
            take_hop(length - 2)
        for h in range(length - 1):
            for way in (0, 1):
                copy, sends, _ = hop(way, h)
                pl.when(sends)(copy.wait_send)
        for place in range(length):
            copy = forward(
                2 * place, other, False, side_send.at[place], side_recv.at[place]
            )
            copy.wait()
    for copy in own_copies:
        copy.wait()
    for copy in copies:
        copy.wait()


def flag_kernel(
    columns, targets_count, capacity, screen_ref, out_ref, send, recv, send_sems, recv_sems
):
    col = lax.axis_index("aux")
    barrier = pltpu.get_barrier_semaphore()
    for k in range(1, columns):
        pl.semaphore_signal(
            barrier, inc=1, device_id={"aux": lax.rem(col + k, columns)}, device_id_type=MESH
        )
    targets = screen_ref[...]
    beyond = jnp.zeros((targets.shape[0], 1), jnp.float32)
    for t in range(targets_count):
        named = jnp.sum(jnp.where(targets == t, 1.0, 0.0), axis=1, keepdims=True)
        beyond += jnp.maximum(named - capacity, 0.0)
    worst = jnp.zeros(out_ref.shape, jnp.float32) + jnp.max(beyond, axis=0, keepdims=True)
    send[...] = worst
    pl.semaphore_wait(barrier, columns - 1)
    copies = []
    for k in range(1, columns):
        copy = pltpu.make_async_remote_copy(
            src_ref=send,
            dst_ref=recv.at[k - 1],
            send_sem=send_sems.at[k],
            recv_sem=recv_sems.at[k],
            device_id={"aux": lax.rem(col + k, columns)},
            device_id_type=MESH,
        )
        copy.start()
        copies.append(copy)
    for k, copy in enumerate(copies):
        copy.wait()
        worst = jnp.maximum(worst, recv[k])
    out_ref[...] = worst


def fit_kernel(
    block_count,
    orbitals,
    entries,
    weights,
    metric_hi,
    metric_lo,
    recv_buf,
    fitted_ref,
    gram_ref,
    coeff,
):
    width = recv_buf.shape[1]
    basis = block_count * width
    chunks, _, wide = coeff.shape
    groups = orbitals // IG
    depth = QG * width
    lanes = QG * IG
    found = entries[0, entries.shape[1] - 1]
    coeff[...] = jnp.zeros_like(coeff)

    def add(k):
        entry, mu, nu = entries[0, k], entries[1, k], entries[2, k]
        block = recv_buf[entry]
        stacked = jnp.concatenate(
            [block[:, c * depth : (c + 1) * depth] for c in range(chunks)], axis=0
        )
        half = jnp.dot(stacked, weights[nu], preferred_element_type=jnp.float32)
        rows = pl.ds(pl.multiple_of(mu * width, width), width)
        for c in range(chunks):
            coeff[c, rows, :] += half[c * width : (c + 1) * width, :]

    def add_two(j, _):
        add(2 * j)
        add(2 * j + 1)
        return 0

    lax.fori_loop(0, (found + 1) // 2, add_two, 0)

    source = iota((wide, wide), 0)
    dest = iota((wide, wide), 1)
    wanted = (
        (dest % orbitals) // IG * lanes + dest // orbitals * IG + dest % IG
    )
    order = (source == wanted).astype(jnp.bfloat16)
    step = min(256, basis)
    for r in range(0, basis, step):
        parts = []
        for g in range(groups):
            piece = jnp.concatenate(
                [coeff[c, r : r + step, g * lanes : (g + 1) * lanes] for c in range(chunks)],
                axis=1,
            ).astype(jnp.bfloat16)
            out = jnp.dot(piece, metric_hi[...], preferred_element_type=jnp.float32)
            out += jnp.dot(piece, metric_lo[...], preferred_element_type=jnp.float32)
            parts.append(out.astype(jnp.bfloat16))
        for o in range(chunks):
            mixed = jnp.concatenate(
                [part[:, o * lanes : (o + 1) * lanes] for part in parts], axis=1
            )
            fitted_ref[0, r : r + step, o * wide : (o + 1) * wide] = jnp.dot(
                mixed, order, preferred_element_type=jnp.float32
            ).astype(jnp.bfloat16)
    gram_ref[...] = lax.dot_general(
        fitted_ref[0],
        fitted_ref[0],
        (((1,), (1,)), ((), ())),
        preferred_element_type=jnp.float32,
    )


def reduce_kernel(
    n,
    columns,
    norm_factor,
    gram_ref,
    out_ref,
    send_one,
    recv_one,
    partial,
    send_two,
    recv_two,
    send_one_sems,
    recv_one_sems,
    send_two_sems,
    recv_two_sems,
):
    me = lax.axis_index("pair")
    col = lax.axis_index("aux")
    barrier = pltpu.get_barrier_semaphore()
    for k in range(1, columns):
        pl.semaphore_signal(
            barrier, inc=1, device_id={"aux": lax.rem(col + k, columns)}, device_id_type=MESH
        )
    for k in range(1, n):
        pl.semaphore_signal(
            barrier, inc=1, device_id={"pair": lax.rem(me + k, n)}, device_id_type=MESH
        )
    for a in range(columns):
        send_one[a] = gram_ref[:, a].astype(send_one.dtype)
    pl.semaphore_wait(barrier, columns + n - 2)
    copies = []
    for k in range(1, columns):
        dst = lax.rem(col + k, columns)
        copy = pltpu.make_async_remote_copy(
            src_ref=send_one.at[dst],
            dst_ref=recv_one.at[k - 1],
            send_sem=send_one_sems.at[k],
            recv_sem=recv_one_sems.at[k],
            device_id={"aux": dst},
            device_id_type=MESH,
        )
        copy.start()
        copies.append(copy)
    total = gram_ref[:, col]
    for k, copy in enumerate(copies):
        copy.wait()
        total += recv_one[k].astype(jnp.float32)
    partial[...] = total
    send_two[...] = total.astype(send_two.dtype)
    copies = []
    for k in range(1, n):
        dst = lax.rem(me + k, n)
        copy = pltpu.make_async_remote_copy(
            src_ref=send_two.at[dst],
            dst_ref=recv_two.at[k - 1],
            send_sem=send_two_sems.at[k],
            recv_sem=recv_two_sems.at[k],
            device_id={"pair": dst},
            device_id_type=MESH,
        )
        copy.start()
        copies.append(copy)
    total = partial[me]
    for k, copy in enumerate(copies):
        copy.wait()
        total += recv_two[k].astype(jnp.float32)
    out_ref[...] = total * norm_factor


def shards(three_center, panel, metric, screen, pair_blocks):
    pair_count = lax.axis_size("pair")
    column_count = lax.axis_size("aux")
    slot_count, width, flat = three_center.shape
    aux = metric.shape[1]
    orbitals = panel.shape[1]
    capacity = max(2, 2 * slot_count // pair_count)
    rows = pair_count * capacity
    basis = pair_count * panel.shape[0]
    block_count = basis // width
    table = (screen[:, :, 0] * block_count + pair_blocks[:, :, 0]) * block_count
    table += pair_blocks[:, :, 1]
    smem = pl.BlockSpec(memory_space=pltpu.SMEM)
    vmem = pl.BlockSpec(memory_space=pltpu.VMEM)
    hbm = pl.BlockSpec(memory_space=pl.ANY)

    size = aux * IG
    depth, wide = QG * width, QG * orbitals

    def fit(part, spill, table, three_center, panel, metric):
        packed, entries = pl.pallas_call(
            functools.partial(pack_kernel, pair_count, part, spill, block_count),
            out_shape=(
                jax.ShapeDtypeStruct((pair_count * part + spill, width, flat), jnp.bfloat16),
                jax.ShapeDtypeStruct((3, rows + 2), jnp.int32),
            ),
            in_specs=[smem, hbm],
            out_specs=(vmem, smem),
            scratch_shapes=[
                pltpu.SMEM((pair_count,), jnp.int32),
                pltpu.SemaphoreType.DMA((slot_count,)),
            ],
            compiler_params=pltpu.CompilerParams(vmem_limit_bytes=16 * 2**20),
            name="pack",
        )(table, three_center)

        received, weights, metric_hi, metric_lo = pl.pallas_call(
            functools.partial(exchange_kernel, pair_count, part, spill),
            out_shape=(
                jax.ShapeDtypeStruct((pair_count * (part + spill), width, flat), jnp.bfloat16),
                jax.ShapeDtypeStruct((block_count, depth, wide), jnp.bfloat16),
                jax.ShapeDtypeStruct((size, size), jnp.bfloat16),
                jax.ShapeDtypeStruct((size, size), jnp.bfloat16),
            ),
            in_specs=[vmem, vmem, vmem],
            out_specs=(vmem, vmem, vmem, vmem),
            scratch_shapes=[
                pltpu.VMEM((basis, orbitals), jnp.bfloat16),
                pltpu.SemaphoreType.DMA((pair_count,)),
                pltpu.SemaphoreType.DMA((pair_count,)),
                pltpu.SemaphoreType.DMA((pair_count,)),
                pltpu.SemaphoreType.DMA((pair_count,)),
                pltpu.SemaphoreType.DMA,
                pltpu.SemaphoreType.DMA,
                pltpu.SemaphoreType.DMA((pair_count,)),
                pltpu.SemaphoreType.DMA((pair_count,)),
                pltpu.SemaphoreType.DMA((pair_count,)),
                pltpu.SemaphoreType.DMA((pair_count,)),
            ],
            compiler_params=pltpu.CompilerParams(
                collective_id=2 if spill else 0, has_side_effects=True, vmem_limit_bytes=28 * 2**20
            ),
            name="exchange_blocks",
        )(packed, panel, metric)

        fitted, gram = pl.pallas_call(
            functools.partial(fit_kernel, block_count, orbitals),
            out_shape=(
                jax.ShapeDtypeStruct((1, basis, aux * orbitals), jnp.bfloat16),
                jax.ShapeDtypeStruct((basis, basis), jnp.float32),
            ),
            in_specs=[smem, vmem, vmem, vmem, vmem],
            out_specs=(vmem, vmem),
            scratch_shapes=[
                pltpu.VMEM((aux // QG, basis + width, wide), jnp.float32),
            ],
            compiler_params=pltpu.CompilerParams(vmem_limit_bytes=33 * 2**20),
            name="fit",
        )(entries, weights, metric_hi, metric_lo, received)
        return fitted, gram

    arrays = (table, three_center, panel, metric)
    direct, spill = 5 * capacity // 8, 3 * slot_count // 16
    if capacity < 8 or pair_count % 2:
        fitted, gram = fit(capacity, 0, *arrays)
    else:
        worst = pl.pallas_call(
            functools.partial(flag_kernel, column_count, pair_count, direct),
            out_shape=jax.ShapeDtypeStruct((8, 128), jnp.float32),
            in_specs=[vmem],
            out_specs=vmem,
            scratch_shapes=[
                pltpu.VMEM((8, 128), jnp.float32),
                pltpu.VMEM((column_count - 1, 8, 128), jnp.float32),
                pltpu.SemaphoreType.DMA((column_count,)),
                pltpu.SemaphoreType.DMA((column_count,)),
            ],
            compiler_params=pltpu.CompilerParams(collective_id=3, has_side_effects=True),
            name="most_beyond",
        )(screen[:, :, 0])
        fitted, gram = lax.cond(
            worst[0, 0] <= spill,
            functools.partial(fit, direct, spill),
            functools.partial(fit, capacity, 0),
            *arrays,
        )

    norm_factor = 1.0 / (pair_count * column_count * aux * orbitals)
    part = basis // (pair_count * column_count)
    exchange = pl.pallas_call(
        functools.partial(reduce_kernel, pair_count, column_count, norm_factor),
        out_shape=jax.ShapeDtypeStruct((part, basis), jnp.float32),
        in_specs=[vmem],
        out_specs=vmem,
        scratch_shapes=[
            pltpu.VMEM((column_count, pair_count, part, basis), jnp.bfloat16),
            pltpu.VMEM((column_count - 1, pair_count, part, basis), jnp.bfloat16),
            pltpu.VMEM((pair_count, part, basis), jnp.float32),
            pltpu.VMEM((pair_count, part, basis), jnp.bfloat16),
            pltpu.VMEM((pair_count - 1, part, basis), jnp.bfloat16),
            pltpu.SemaphoreType.DMA((column_count,)),
            pltpu.SemaphoreType.DMA((column_count,)),
            pltpu.SemaphoreType.DMA((pair_count,)),
            pltpu.SemaphoreType.DMA((pair_count,)),
        ],
        compiler_params=pltpu.CompilerParams(
            collective_id=1, has_side_effects=True, vmem_limit_bytes=24 * 2**20
        ),
        name="reduce_rows",
    )(gram.reshape(pair_count, column_count, part, basis))
    return fitted, exchange


def solution(mesh):
    return jax.shard_map(
        shards,
        mesh=mesh,
        in_specs=(
            P(("pair", "aux"), None, None),
            P("pair", None),
            P(("pair", "aux"), None, None),
            P(None, "aux", None),
            P(None, "aux", None),
        ),
        out_specs=(P(("pair", "aux"), None, None), P(("pair", "aux"), None)),
        check_vma=False,
    )
```
